32 devices in a mesh: grp: 2 (over y), pan: 4 (over z), en: 4 (over x, core).
Axes of the slice: x: 2, y: 2, z: 4, core: 2. Of those that a mesh axis runs over, the one named last changes fastest.
Arguments:
- retarded: float32 [2, 8, 2048, 2048], P(None, ('grp', 'en'), 'pan'), parts along dimension 1, may hold values from -0.75 to 0.75
- contact: float32 [2, 8, 2048, 128], P(None, ('grp', 'en'), 'pan'), parts along dimension 1, may hold values from -6 to 6
- atom_kind: int32 [256], replicated, may hold values from 0 to 3
- coupling: float32 [4, 3], replicated, may hold values from 0.2 to 1
- shifts: int32 [3], replicated, may hold values from 1 to 3, as said below
Outputs:
- lesser_diag: float32 [2, 8, 2048, 128], P(None, ('grp', 'en'), 'pan'), parts along dimension 1
- lesser_upper: float32 [2, 8, 2048, 128], P(None, ('grp', 'en'), 'pan'), parts along dimension 1
- sigma_next: float32 [2, 8, 2048, 128], P(None, ('grp', 'en'), 'pan'), parts along dimension 1
The draws below stay inside these ranges and needn't reach their ends.
There are 2 independent parts, one for each index of `grp`. The reference program is written for one: setup_inputs(seed, part) draws one part's arguments, and reference() takes and returns one part's arrays. A program takes and returns all parts, laid end to end along the dimension named above; an argument that names none is the same for every part. Nothing has to cross between parts.
Inputs may be any that keep to these rules, and one draw needn't show every extreme that they name: `shifts`: the three entries are distinct: one is 1, one is 3, and one lies strictly between them.
All inputs are finite; a program needn't handle non-finite values.
Results may differ from the reference program's by a relative error of at most 0.0001.
Values sent between devices are 32-bit elements; how exact they have to be, the bound alone decides.
A program may use at most 128 MiB of HBM per device.

```python
import math
import jax
import jax.numpy as jnp
from jax import lax

N = 2048
B = 128
ORB = 8
KINDS = 4
MODES = 3
ITERS = 2
ENERGIES = 4
ATOMS = 256


def draw_shifts(key, part):
    order_key = jax.random.fold_in(key, 71)
    middle_key = jax.random.fold_in(key, 72)
    middle = jax.random.randint(middle_key, (), 2, ENERGIES - 1, dtype=jnp.int32)
    values = jnp.stack([jnp.array(1, jnp.int32), middle, jnp.array(ENERGIES - 1, jnp.int32)])
    order = jax.random.permutation(order_key, 3)
    return values[order].astype(jnp.int32)


def place_ends(result, own_key, smallest, largest):
    spot = [jax.random.randint(jax.random.fold_in(own_key, axis), (), 0, length) for axis, length in enumerate(result.shape)]
    main_axis = result.shape.index(max(result.shape))
    next_to = spot[:main_axis] + [(spot[main_axis] + 1) % result.shape[main_axis]] + spot[main_axis + 1:]
    return result.at[tuple(spot)].set(smallest).at[tuple(next_to)].set(largest)


def steps_of(own_key, shape, cuts, low, high):
    gain, own = 1.0, jax.random.fold_in(own_key, 6)
    for position, blocks in cuts:
        draws = jnp.exp(jax.random.uniform(jax.random.fold_in(own, position), (blocks,), jnp.float32, low / len(cuts), high / len(cuts)))
        gain = gain * jnp.repeat(draws, shape[position] // blocks).reshape([-1 if axis == position else 1 for axis in range(len(shape))])
    return gain


def normal_values(rng, shape, width, limit, shards=(), kind=jnp.bfloat16):
    result = width * jax.random.normal(rng, shape, jnp.float32)
    if shards:
        result = result * steps_of(rng, shape, shards, -0.22, 0.18)
    return jnp.clip(result, -limit, limit).astype(kind)


def setup_inputs(seed: int = 0, part: int = 0) -> dict:
    seeds = jax.random.split(jax.random.key(seed), 6)
    part_keys = jax.random.split(jax.random.fold_in(seeds[5], part), 6)
    return {
        "retarded": normal_values(part_keys[0], (2, ENERGIES, N, N), 0.125, 0.75, ((1, 4), (2, 4)), jnp.float32),
        "contact": normal_values(part_keys[1], (2, ENERGIES, N, B), 1.0, 6.0, ((1, 4), (2, 4)), jnp.float32),
        "atom_kind": place_ends(jax.random.randint(seeds[2], (ATOMS,), 0, KINDS), jax.random.fold_in(seeds[2], 1), 0, KINDS - 1).astype(jnp.int32),
        "coupling": jnp.clip(jnp.exp(jax.random.uniform(seeds[3], (KINDS, MODES), jnp.float32, math.log(0.2), math.log(1.0))), 0.2, 1.0),
        "shifts": draw_shifts(jax.random.fold_in(seeds[5], 71), part),
    }


precise = lax.Precision.HIGHEST

def mix_plain(blocks):
    return jnp.stack([jnp.stack([blocks[0], blocks[1]]), jnp.stack([-blocks[1], blocks[0]])])

def mix_conj(blocks):
    return jnp.stack([jnp.stack([blocks[0], -blocks[1]]), jnp.stack([blocks[1], blocks[0]])])

def blocked(green_cols, blocks):
    return jnp.einsum('a...rkq,ac...kqj->c...rkj', green_cols, mix_plain(blocks), precision=precise)

def adjoint_product(left_side, right_mixed):
    return jnp.einsum('a...rn,ac...sn->c...rs', left_side, right_mixed, precision=precise)

def coupling_factor(atom_kind, coupling):
    onehot = (atom_kind[:, None] == jnp.arange(coupling.shape[0], dtype=jnp.int32)[None, :]).astype(jnp.float32)
    per_atom = jnp.dot(onehot, coupling, precision=precise, preferred_element_type=jnp.float32)
    per_orbital = jnp.repeat(per_atom, ORB, axis=0)
    per_column = jnp.repeat(per_orbital.reshape(N // B, B, coupling.shape[1]), B, axis=0)
    return per_orbital[:, None, :] * per_column

def energy_table(shifts, levels):
    energy = jnp.arange(levels, dtype=jnp.int32)
    target = energy[None, :, None]
    source = energy[None, None, :]
    offsets = shifts[:, None, None]
    return ((source == target + offsets) | (source == target - offsets)).astype(jnp.float32)

def phonon(lesser_diag, shift_table, factor):
    shifted = jnp.einsum('mef,cfrb->mcerb', shift_table, lesser_diag, precision=precise)
    return jnp.einsum('mcerb,rbm->cerb', shifted, factor, precision=precise)

def lesser(energy_pair):
    retard_one, sigma_one = energy_pair
    blocks = N // B
    block_scale = 1.0 / math.sqrt(B)
    product = blocked(retard_one.reshape(2, N, blocks, B), sigma_one.reshape(2, blocks, B, B)).reshape(2, N, N)
    prod_rows = product.reshape(2, blocks, B, N)
    retard_mixed = mix_conj(retard_one.reshape(2, blocks, B, N))
    diagonal = adjoint_product(prod_rows, retard_mixed) * block_scale
    upper_part = adjoint_product(prod_rows[:, :-1], retard_mixed[:, :, 1:]) * block_scale
    upper_part = jnp.concatenate([upper_part, jnp.zeros((2, 1, B, B), jnp.float32)], axis=1)
    return (diagonal.reshape(2, N, B), upper_part.reshape(2, N, B))

def reference(retarded, contact, atom_kind, coupling, shifts):
    factor = coupling_factor(atom_kind, coupling)
    shift_table = energy_table(shifts, ENERGIES)
    moved_green = jnp.moveaxis(retarded, 1, 0)
    self_energy = contact
    for rounds in range(ITERS):
        diag_all, upper_all = lax.map(lesser, (moved_green, jnp.moveaxis(self_energy, 1, 0)))
        lesser_diag = jnp.moveaxis(diag_all, 0, 1)
        lesser_upper = jnp.moveaxis(upper_all, 0, 1)
        self_energy = contact + phonon(lesser_diag, shift_table, factor)
    return (lesser_diag, lesser_upper, self_energy)
```

```python
import functools
import math

import jax
import jax.numpy as jnp
from jax import lax
from jax.experimental import pallas as pl
from jax.experimental.pallas import tpu as pltpu
from jax.sharding import PartitionSpec as P

B = 128
ORB = 8
ITERS = 2
MESH = pl.DeviceIdType.MESH


def split(x):
    hi = x.astype(jnp.bfloat16)
    return hi, (x - hi.astype(jnp.float32)).astype(jnp.bfloat16)


def nn(a, b):
    return jnp.dot(a, b, preferred_element_type=jnp.float32)


def nt(a, b):
    return lax.dot_general(a, b, (((1,), (1,)), ((), ())), preferred_element_type=jnp.float32)


def three(f, a, b):
    return f(a[0], b[0]) + (f(a[1], b[0]) + f(a[0], b[1]))


def kernel(
    n, energies, L, modes,
    green, contact, ccol, crow, shifts,
    diag_out, upper_out, sigma_out,
    gst, rhi, rlo, zbuf, gnext, gprev, dacc, uacc, uret, uadd, dbuf, sib, xsend, xrecv,
    gsem, zs, zr, ns, nr, ps, pr, us, ur, ss, sr, xs, xr,
):
    NB = n * L
    rows = L * B
    X = energies // 2
    scale = 1.0 / math.sqrt(B)
    z = lax.axis_index("pan")
    e = lax.axis_index("en")
    x = lax.div(e, 2)
    core = lax.rem(e, 2)
    other = x * 2 + 1 - core

    load = pltpu.make_async_copy(green.at[:, 0], gst, gsem)
    load.start()
    zbuf[0, pl.ds(z * L, L)] = jnp.swapaxes(contact[:, 0].reshape(2, L, B, B), 0, 1)

    barrier = pltpu.get_barrier_semaphore()

    @pl.when(z > 0)
    def _():
        pl.semaphore_signal(barrier, inc=1, device_id={"pan": z - 1}, device_id_type=MESH)

    @pl.when(z < n - 1)
    def _():
        pl.semaphore_signal(barrier, inc=1, device_id={"pan": z + 1}, device_id_type=MESH)

    pl.semaphore_signal(barrier, inc=1, device_id={"en": other}, device_id_type=MESH)

    def target(dx):
        return lax.rem(x + dx, X) * 2 + core

    for dx in range(1, X):
        pl.semaphore_signal(barrier, inc=1, device_id={"en": target(dx)}, device_id_type=MESH)

    ends = (z > 0).astype(jnp.int32) + (z < n - 1).astype(jnp.int32)
    pl.semaphore_wait(barrier, X + ends)

    def zcopy(it, k, side):
        return pltpu.make_async_remote_copy(
            src_ref=zbuf.at[it, k], dst_ref=zbuf.at[it, k],
            send_sem=zs.at[it, side, k], recv_sem=zr.at[it, k],
            device_id={"pan": z + 1 - 2 * side}, device_id_type=MESH,
        )

    def send_own(it, b):
        k = z * L + b

        @pl.when(z < n - 1)
        def _():
            zcopy(it, k, 0).start()

        @pl.when(z > 0)
        def _():
            zcopy(it, k, 1).start()

    def cols(k):
        return pl.ds(pl.multiple_of(k * B, B), B)

    def cut(p):
        return lax.div(p * NB, max(n - 2, 1)) if n > 2 else p * 0 + NB // 2

    cut_here = cut(z)
    cut_before = cut(jnp.maximum(z - 1, 0))

    def next_copy(k):
        return pltpu.make_async_remote_copy(
            src_ref=gst.at[:, pl.ds(0, B), cols(k)], dst_ref=gnext.at[k],
            send_sem=ns.at[k], recv_sem=nr.at[k],
            device_id={"pan": z - 1}, device_id_type=MESH,
        )

    def prev_copy(k):
        return pltpu.make_async_remote_copy(
            src_ref=gst.at[:, pl.ds(rows - B, B), cols(k)], dst_ref=gprev.at[k],
            send_sem=ps.at[k], recv_sem=pr.at[k],
            device_id={"pan": z + 1}, device_id_type=MESH,
        )

    def next_sent(k):
        return jnp.logical_and(z > 0, k < cut_before)

    def prev_sent(k):
        return jnp.logical_and(z < n - 1, k >= cut_here)

    def send_edge(k):
        @pl.when(next_sent(k))
        def _():
            next_copy(k).start()

        @pl.when(prev_sent(k))
        def _():
            prev_copy(k).start()

    def absorb(it, k):
        if it == 0:
            cat = jnp.concatenate([gst[0, :, cols(k)], gst[1, :, cols(k)]], axis=1)
            hi, lo = split(cat)
            for part, ref in ((hi, rhi), (lo, rlo)):
                ref[k, :, :B, :] = part.reshape(L, B, 2 * B)
                ref[k, :, B:, :] = jnp.concatenate(
                    [-part[:, B:], part[:, :B]], axis=1
                ).reshape(L, B, 2 * B)
            left = (hi, lo)
        else:
            left = tuple(ref[k, :, :B, :].reshape(rows, 2 * B) for ref in (rhi, rlo))
        re, im = zbuf[it, k, 0], zbuf[it, k, 1]
        mixed = split(
            jnp.concatenate(
                [jnp.concatenate([re, im], axis=1), jnp.concatenate([-im, re], axis=1)], axis=0
            )
        )
        prod = split(three(nn, left, mixed))
        for j in range(L):
            right = (rhi[k, j], rlo[k, j])
            if it < ITERS - 1 or j == 0:
                got = three(nt, tuple(p[j * B:(j + 1) * B] for p in prod), right)
                dacc[j] += got
            else:
                got = three(nt, tuple(p[(j - 1) * B:(j + 1) * B] for p in prod), right)
                uacc[j - 1] += got[:B]
                dacc[j] += got[B:]
        if it == ITERS - 1:
            @pl.when(jnp.logical_and(z < n - 1, k < cut_here))
            def _():
                next_copy(k).wait_recv()
                gr, gi = gnext[k, 0], gnext[k, 1]
                right = split(
                    jnp.concatenate(
                        [jnp.concatenate([gr, gi], axis=1), jnp.concatenate([-gi, gr], axis=1)],
                        axis=0,
                    )
                )
                uacc[L - 1] += three(nt, tuple(p[rows - B:] for p in prod), right)

            @pl.when(jnp.logical_and(z > 0, k >= cut_before))
            def _():
                prev_copy(k).wait_recv()
                edge = split(jnp.concatenate([gprev[k, 0], gprev[k, 1]], axis=1))
                edge = split(three(nn, edge, mixed))
                uret[...] += three(nt, edge, (rhi[k, 0], rlo[k, 0]))

    steps = n * L
    per = -(-NB // max(steps - 2 * L, 1))

    def gather(it):
        @pl.loop(0, steps)
        def _(u):
            d = lax.div(u, L)
            b = lax.rem(u, L)

            @pl.loop(0, 2)
            def _(side):
                panel = z - d + side * 2 * d
                valid = (panel >= 0) & (panel < n) & ((d > 0) | (side == 0))
                k = panel * L + b

                @pl.when(valid)
                def _():
                    @pl.when(d > 0)
                    def _():
                        zcopy(it, k, side).wait_recv()
                        onward = z + 1 - 2 * side

                        @pl.when((onward >= 0) & (onward < n))
                        def _():
                            zcopy(it, k, side).start()

                    absorb(it, k)

            if it == 0:
                for i in range(per):
                    k = (u - 2 * L) * per + i

                    @pl.when((k >= 0) & (k < NB))
                    def _():
                        send_edge(k)

    def weight(m, target_energy, source):
        gap = shifts[m]
        hit = (source == target_energy + gap) | (source == target_energy - gap)
        return jnp.where(hit, jnp.float32(1.0), jnp.float32(0.0))

    def factor(b, target_energy, source):
        total = None
        for m in range(modes):
            col = ccol[b * B:(b + 1) * B, m:m + 1] * weight(m, target_energy, source)
            term = col * crow[b, m:m + 1, :]
            total = term if total is None else total + term
        return jnp.concatenate([total, total], axis=1)

    def sib_copy(it, b):
        return pltpu.make_async_remote_copy(
            src_ref=dbuf.at[it, b], dst_ref=sib.at[it, b],
            send_sem=ss.at[it, b], recv_sem=sr.at[it, b],
            device_id={"en": other}, device_id_type=MESH,
        )

    def x_copy(it, dx, b):
        return pltpu.make_async_remote_copy(
            src_ref=xsend.at[it, dx - 1, b], dst_ref=xrecv.at[it, dx - 1, b],
            send_sem=xs.at[it, dx - 1, b], recv_sem=xr.at[it, dx - 1, b],
            device_id={"en": target(dx)}, device_id_type=MESH,
        )

    def exchange(it, done):
        for b in range(L):
            dbuf[it, b] = dacc[b] * scale
            sib_copy(it, b).start()
        for b in range(L):
            sib_copy(it, b).wait_recv()
            for dx in range(1, X):
                to = target(dx)
                xsend[it, dx - 1, b] = (
                    factor(b, to, e) * dbuf[it, b] + factor(b, to, other) * sib[it, b]
                )
                x_copy(it, dx, b).start()
        for b in range(L):
            total = factor(b, e, e) * dbuf[it, b] + factor(b, e, other) * sib[it, b]
            for dx in range(1, X):
                x_copy(it, dx, b).wait_recv()
                total = total + xrecv[it, dx - 1, b]
            span = slice(b * B, (b + 1) * B)
            done(b, contact[0, 0, span] + total[:, :B], contact[1, 0, span] + total[:, B:])

    for b in range(L):
        send_own(0, b)
    dacc[...] = jnp.zeros_like(dacc)
    uacc[...] = jnp.zeros_like(uacc)
    uret[...] = jnp.zeros_like(uret)
    load.wait()

    for it in range(ITERS):
        gather(it)
        if it < ITERS - 1:
            def done(b, re, im):
                k = z * L + b
                zbuf[it + 1, k, 0] = re
                zbuf[it + 1, k, 1] = im
                send_own(it + 1, b)

            exchange(it, done)
            dacc[...] = jnp.zeros_like(dacc)

    back = pltpu.make_async_remote_copy(
        src_ref=uret, dst_ref=uadd, send_sem=us, recv_sem=ur,
        device_id={"pan": z - 1}, device_id_type=MESH,
    )

    @pl.when(z > 0)
    def _():
        back.start()

    def final(b, re, im):
        span = slice(b * B, (b + 1) * B)
        sigma_out[0, 0, span] = re
        sigma_out[1, 0, span] = im

    exchange(ITERS - 1, final)

    @pl.when(z < n - 1)
    def _():
        back.wait_recv()
        uacc[L - 1] += uadd[...]

    for b in range(L):
        span = slice(b * B, (b + 1) * B)
        diag_out[0, 0, span] = dbuf[ITERS - 1, b, :, :B]
        diag_out[1, 0, span] = dbuf[ITERS - 1, b, :, B:]
        upper_out[0, 0, span] = uacc[b, :, :B] * scale
        upper_out[1, 0, span] = uacc[b, :, B:] * scale

    @pl.when(z > 0)
    def _():
        back.wait_send()

    for it in range(ITERS):
        for b in range(L):
            sib_copy(it, b).wait_send()
            for dx in range(1, X):
                x_copy(it, dx, b).wait_send()

    @pl.loop(0, NB)
    def _(k):
        panel = lax.div(k, L)
        for it in range(ITERS):
            @pl.when((panel <= z) & (z < n - 1))
            def _():
                zcopy(it, k, 0).wait_send()

            @pl.when((panel >= z) & (z > 0))
            def _():
                zcopy(it, k, 1).wait_send()

        @pl.when(next_sent(k))
        def _():
            next_copy(k).wait_send()

        @pl.when(prev_sent(k))
        def _():
            prev_copy(k).wait_send()


def body(n, energies, retarded, contact, atom_kind, coupling, shifts):
    rows, columns = retarded.shape[2:]
    L = rows // B
    NB = n * L
    X = energies // 2
    kinds, modes = coupling.shape
    atoms = rows // ORB
    pan = lax.axis_index("pan")
    mine = lax.dynamic_slice_in_dim(atom_kind, pan * atoms, atoms, 0)
    per_atom = jnp.zeros((atoms, modes), jnp.float32)
    for q in range(kinds):
        per_atom = jnp.where((mine == q)[:, None], coupling[q][None, :], per_atom)
    ccol = jnp.repeat(per_atom, ORB, axis=0)
    crow = jnp.swapaxes(ccol.reshape(L, B, modes), 1, 2)
    f32, bf16 = jnp.float32, jnp.bfloat16
    out = jax.ShapeDtypeStruct(contact.shape, f32)
    vmem = pl.BlockSpec(memory_space=pltpu.VMEM)
    dma = pltpu.SemaphoreType.DMA
    far = max(X - 1, 1)
    return pl.pallas_call(
        functools.partial(kernel, n, energies, L, modes),
        out_shape=(out, out, out),
        in_specs=[
            pl.BlockSpec(memory_space=pl.ANY), vmem, vmem, vmem,
            pl.BlockSpec(memory_space=pltpu.SMEM),
        ],
        out_specs=(vmem, vmem, vmem),
        scratch_shapes=[
            pltpu.VMEM((2, rows, columns), f32),
            pltpu.VMEM((NB, L, 2 * B, 2 * B), bf16),
            pltpu.VMEM((NB, L, 2 * B, 2 * B), bf16),
            pltpu.VMEM((ITERS, NB, 2, B, B), f32),
            pltpu.VMEM((NB, 2, B, B), f32),
            pltpu.VMEM((NB, 2, B, B), f32),
            pltpu.VMEM((L, B, 2 * B), f32),
            pltpu.VMEM((L, B, 2 * B), f32),
            pltpu.VMEM((B, 2 * B), f32),
            pltpu.VMEM((B, 2 * B), f32),
            pltpu.VMEM((ITERS, L, B, 2 * B), f32),
            pltpu.VMEM((ITERS, L, B, 2 * B), f32),
            pltpu.VMEM((ITERS, far, L, B, 2 * B), f32),
            pltpu.VMEM((ITERS, far, L, B, 2 * B), f32),
            dma,
            dma((ITERS, 2, NB)), dma((ITERS, NB)),
            dma((NB,)), dma((NB,)), dma((NB,)), dma((NB,)),
            dma, dma,
            dma((ITERS, L)), dma((ITERS, L)),
            dma((ITERS, far, L)), dma((ITERS, far, L)),
        ],
        compiler_params=pltpu.CompilerParams(
            collective_id=0, has_side_effects=True, vmem_limit_bytes=58 * 2**20
        ),
        cost_estimate=pl.CostEstimate(
            flops=2 * 3 * 20 * rows * columns * B, bytes_accessed=8 * rows * columns,
            transcendentals=0,
        ),
    )(retarded, contact, ccol, crow, shifts)


def solution(mesh):
    shape = dict(mesh.shape)
    spec = P(None, ("grp", "en"), "pan", None)
    return jax.shard_map(
        functools.partial(body, shape["pan"], shape["en"]),
        mesh=mesh,
        in_specs=(spec, spec, P(), P(), P()),
        out_specs=(spec, spec, spec),
        check_vma=False,
    )
```

```python
import functools
import math

import jax
import jax.numpy as jnp
from jax import lax
from jax.experimental import pallas as pl
from jax.experimental.pallas import tpu as pltpu
from jax.sharding import PartitionSpec as P

B = 128
ORB = 8
ITERS = 2
MESH = pl.DeviceIdType.MESH


def split(x):
    hi = x.astype(jnp.bfloat16)
    return hi, (x - hi.astype(jnp.float32)).astype(jnp.bfloat16)


def nn(a, b):
    return jnp.dot(a, b, preferred_element_type=jnp.float32)


def nt(a, b):
    return lax.dot_general(a, b, (((1,), (1,)), ((), ())), preferred_element_type=jnp.float32)


def three(f, a, b):
    return f(a[0], b[0]) + (f(a[1], b[0]) + f(a[0], b[1]))


def mix(re, im):
    return split(
        jnp.concatenate(
            [jnp.concatenate([re, im], axis=1), jnp.concatenate([-im, re], axis=1)], axis=0
        )
    )


def kernel(
    n, energies, L, modes,
    green, contact, atom_kind, coupling, shifts,
    diag_out, upper_out, sigma_out,
    gst, rhi, rlo, fac, phi, plo, zbuf, gnext, gprev, dacc, uacc, uret, uadd, dbuf, sib, xsend, xrecv,
    gsem, csem, zs, zr, ns, nr, ps, pr, us, ur, ss, sr, xs, xr,
):
    NB = n * L
    rows = L * B
    X = energies // 2
    scale = 1.0 / math.sqrt(B)
    z = lax.axis_index("pan")
    e = lax.axis_index("en")
    x = lax.div(e, 2)
    core = lax.rem(e, 2)
    other = x * 2 + 1 - core

    load = pltpu.make_async_copy(green.at[:, 0], gst, gsem)
    load.start()
    own = [
        pltpu.make_async_copy(
            contact.at[:, 0, pl.ds(b * B, B)], zbuf.at[0, z * L + b], csem.at[b]
        )
        for b in range(L)
    ]
    for copy in own:
        copy.start()

    barrier = pltpu.get_barrier_semaphore()

    @pl.when(z > 0)
    def _():
        pl.semaphore_signal(barrier, inc=1, device_id={"pan": z - 1}, device_id_type=MESH)

    @pl.when(z < n - 1)
    def _():
        pl.semaphore_signal(barrier, inc=1, device_id={"pan": z + 1}, device_id_type=MESH)

    pl.semaphore_signal(barrier, inc=1, device_id={"en": other}, device_id_type=MESH)

    def target(dx):
        return lax.rem(x + dx, X) * 2 + core

    for dx in range(1, X):
        pl.semaphore_signal(barrier, inc=1, device_id={"en": target(dx)}, device_id_type=MESH)

    ends = (z > 0).astype(jnp.int32) + (z < n - 1).astype(jnp.int32)
    pl.semaphore_wait(barrier, X + ends)

    def zcopy(it, k, side):
        return pltpu.make_async_remote_copy(
            src_ref=zbuf.at[it, k], dst_ref=zbuf.at[it, k],
            send_sem=zs.at[it, side, k], recv_sem=zr.at[it, k],
            device_id={"pan": z + 1 - 2 * side}, device_id_type=MESH,
        )

    def send_own(it, b):
        k = z * L + b
        if it == 0:
            own[b].wait()

        @pl.when(z < n - 1)
        def _():
            zcopy(it, k, 0).start()

        @pl.when(z > 0)
        def _():
            zcopy(it, k, 1).start()

    def cols(k):
        return pl.ds(pl.multiple_of(k * B, B), B)

    def cut(p):
        return lax.div(p * NB, max(n - 2, 1)) if n > 2 else p * 0 + NB // 2

    cut_here = cut(z)
    cut_before = cut(jnp.maximum(z - 1, 0))

    def next_copy(k):
        return pltpu.make_async_remote_copy(
            src_ref=gst.at[:, pl.ds(0, B), cols(k)], dst_ref=gnext.at[k],
            send_sem=ns.at[k], recv_sem=nr.at[k],
            device_id={"pan": z - 1}, device_id_type=MESH,
        )

    def prev_copy(k):
        return pltpu.make_async_remote_copy(
            src_ref=gst.at[:, pl.ds(rows - B, B), cols(k)], dst_ref=gprev.at[k],
            send_sem=ps.at[k], recv_sem=pr.at[k],
            device_id={"pan": z + 1}, device_id_type=MESH,
        )

    def next_sent(k):
        return jnp.logical_and(z > 0, k < cut_before)

    def prev_sent(k):
        return jnp.logical_and(z < n - 1, k >= cut_here)

    at_end = ((z == 0) | (z == n - 1)).astype(jnp.int32)

    def paced(it, u):
        fast = lax.div(3 * jnp.maximum(u + 1 - 2 * L, 0), 2)
        slow = jnp.maximum(u + 1 - (n - 1) * L, 0)
        first = at_end * fast + (1 - at_end) * slow
        if it == 0:
            return jnp.minimum(first, NB)
        most = at_end * lax.div(3 * (n - 2) * L, 2) + (1 - at_end) * L
        later = at_end * jnp.maximum(u + 1 - L, 0) + (1 - at_end) * jnp.maximum(u + 1 - 2 * L, 0)
        return jnp.minimum(most + later, NB)

    def send_edge(begin, end):
        @pl.loop(begin, end)
        def _(i):
            right = cut_here + i

            @pl.when((z > 0) & (i < cut_before))
            def _():
                next_copy(i).start()

            @pl.when((z < n - 1) & (right < NB))
            def _():
                prev_copy(right).start()

    def absorb(it, k):
        if it == 0:
            cat = jnp.concatenate([gst[0, :, cols(k)], gst[1, :, cols(k)]], axis=1)
            hi, lo = split(cat)
            for part, ref in ((hi, rhi), (lo, rlo)):
                ref[k, :, :B, :] = part.reshape(L, B, 2 * B)
                ref[k, :, B:, :] = jnp.concatenate(
                    [-part[:, B:], part[:, :B]], axis=1
                ).reshape(L, B, 2 * B)
            left = (hi, lo)
        else:
            left = tuple(ref[k, :, :B, :].reshape(rows, 2 * B) for ref in (rhi, rlo))
        mixed = mix(zbuf[it, k, 0], zbuf[it, k, 1])
        prod = split(three(nn, left, mixed))
        for j in range(L):
            right = (rhi[k, j], rlo[k, j])
            if it < ITERS - 1 or j == 0:
                got = three(nt, tuple(p[j * B:(j + 1) * B] for p in prod), right)
                dacc[j] += got
            else:
                got = three(nt, tuple(p[(j - 1) * B:(j + 1) * B] for p in prod), right)
                uacc[j - 1] += got[:B]
                dacc[j] += got[B:]
        if it == ITERS - 1:
            phi[k] = prod[0][rows - B:]
            plo[k] = prod[1][rows - B:]

    def edges():
        @pl.loop(0, NB)
        def _(k):
            @pl.when((z < n - 1) & (k < cut_here))
            def _():
                next_copy(k).wait_recv()
                gr, gi = gnext[k, 0], gnext[k, 1]
                right = split(
                    jnp.concatenate(
                        [jnp.concatenate([gr, gi], axis=1), jnp.concatenate([-gi, gr], axis=1)],
                        axis=0,
                    )
                )
                uacc[L - 1] += three(nt, (phi[k], plo[k]), right)

            @pl.when((z > 0) & (k >= cut_before))
            def _():
                prev_copy(k).wait_recv()
                edge = split(jnp.concatenate([gprev[k, 0], gprev[k, 1]], axis=1))
                edge = split(three(nn, edge, mix(zbuf[ITERS - 1, k, 0], zbuf[ITERS - 1, k, 1])))
                uret[...] += three(nt, edge, (rhi[k, 0], rlo[k, 0]))

    steps = n * L

    def gather(it):
        @pl.loop(0, steps)
        def _(u):
            d = lax.div(u, L)
            b = lax.rem(u, L)

            @pl.loop(0, 2)
            def _(side):
                panel = z - d + side * 2 * d
                valid = (panel >= 0) & (panel < n) & ((d > 0) | (side == 0))
                k = panel * L + b

                @pl.when(valid)
                def _():
                    @pl.when(d > 0)
                    def _():
                        zcopy(it, k, side).wait_recv()
                        onward = z + 1 - 2 * side

                        @pl.when((onward >= 0) & (onward < n))
                        def _():
                            zcopy(it, k, side).start()

                    absorb(it, k)

            begin = paced(it, u - 1)
            if it == ITERS - 1:
                begin = jnp.where(u == 0, paced(0, steps - 1), begin)
            send_edge(begin, paced(it, u))

        if it == ITERS - 1:
            send_edge(paced(it, steps - 1), NB)

    def weight(m, target_energy, source):
        gap = shifts[m]
        hit = (source == target_energy + gap) | (source == target_energy - gap)
        return jnp.where(hit, jnp.float32(1.0), jnp.float32(0.0))

    def factor(b, target_energy, source):
        total = sum(fac[m, b] * weight(m, target_energy, source) for m in range(modes))
        return jnp.concatenate([total, total], axis=1)

    def make_factor():
        per_block = B // ORB
        lane_atom = lax.div(lax.broadcasted_iota(jnp.int32, (ORB, B), 1), ORB)

        @pl.loop(0, L)
        def _(b):
            kinds = [atom_kind[(z * L + b) * per_block + a] for a in range(per_block)]
            for m in range(modes):
                values = [coupling[kind, m] for kind in kinds]
                row = jnp.zeros((ORB, B), jnp.float32)
                for a, value in enumerate(values):
                    row = jnp.where(lane_atom == a, value, row)
                for a, value in enumerate(values):
                    fac[m, b, a * ORB:(a + 1) * ORB, :] = value * row

    def sib_copy(it, b):
        return pltpu.make_async_remote_copy(
            src_ref=dbuf.at[it, b], dst_ref=sib.at[it, b],
            send_sem=ss.at[it, b], recv_sem=sr.at[it, b],
            device_id={"en": other}, device_id_type=MESH,
        )

    def x_copy(it, dx, b):
        return pltpu.make_async_remote_copy(
            src_ref=xsend.at[it, dx - 1, b], dst_ref=xrecv.at[it, dx - 1, b],
            send_sem=xs.at[it, dx - 1, b], recv_sem=xr.at[it, dx - 1, b],
            device_id={"en": target(dx)}, device_id_type=MESH,
        )

    def exchange(it, done, between):
        for b in range(L):
            dbuf[it, b] = dacc[b] * scale
            sib_copy(it, b).start()
        for b in range(L):
            sib_copy(it, b).wait_recv()
            for dx in range(1, X):
                to = target(dx)
                xsend[it, dx - 1, b] = (
                    factor(b, to, e) * dbuf[it, b] + factor(b, to, other) * sib[it, b]
                )
                x_copy(it, dx, b).start()
        between()
        for b in range(L):
            total = factor(b, e, e) * dbuf[it, b] + factor(b, e, other) * sib[it, b]
            for dx in range(1, X):
                x_copy(it, dx, b).wait_recv()
                total = total + xrecv[it, dx - 1, b]
            k = z * L + b
            done(b, zbuf[0, k, 0] + total[:, :B], zbuf[0, k, 1] + total[:, B:])

    for b in range(L):
        send_own(0, b)
    dacc[...] = jnp.zeros_like(dacc)
    uacc[...] = jnp.zeros_like(uacc)
    uret[...] = jnp.zeros_like(uret)
    make_factor()
    load.wait()

    for it in range(ITERS):
        gather(it)
        if it < ITERS - 1:
            def done(b, re, im):
                k = z * L + b
                zbuf[it + 1, k, 0] = re
                zbuf[it + 1, k, 1] = im
                send_own(it + 1, b)

            exchange(it, done, lambda: None)
            dacc[...] = jnp.zeros_like(dacc)

    back = pltpu.make_async_remote_copy(
        src_ref=uret, dst_ref=uadd, send_sem=us, recv_sem=ur,
        device_id={"pan": z - 1}, device_id_type=MESH,
    )

    def between():
        edges()

        @pl.when(z > 0)
        def _():
            back.start()

    def final(b, re, im):
        span = slice(b * B, (b + 1) * B)
        sigma_out[0, 0, span] = re
        sigma_out[1, 0, span] = im

    exchange(ITERS - 1, final, between)

    @pl.when(z < n - 1)
    def _():
        back.wait_recv()
        uacc[L - 1] += uadd[...]

    for b in range(L):
        span = slice(b * B, (b + 1) * B)
        diag_out[0, 0, span] = dbuf[ITERS - 1, b, :, :B]
        diag_out[1, 0, span] = dbuf[ITERS - 1, b, :, B:]
        upper_out[0, 0, span] = uacc[b, :, :B] * scale
        upper_out[1, 0, span] = uacc[b, :, B:] * scale

    @pl.when(z > 0)
    def _():
        back.wait_send()

    for it in range(ITERS):
        for b in range(L):
            sib_copy(it, b).wait_send()
            for dx in range(1, X):
                x_copy(it, dx, b).wait_send()

    @pl.loop(0, NB)
    def _(k):
        panel = lax.div(k, L)
        for it in range(ITERS):
            @pl.when((panel <= z) & (z < n - 1))
            def _():
                zcopy(it, k, 0).wait_send()

            @pl.when((panel >= z) & (z > 0))
            def _():
                zcopy(it, k, 1).wait_send()

        @pl.when(next_sent(k))
        def _():
            next_copy(k).wait_send()

        @pl.when(prev_sent(k))
        def _():
            prev_copy(k).wait_send()


def place(diag, upper, sigma, diag_out, upper_out, sigma_out):
    diag_out[...] = diag[...]
    upper_out[...] = upper[...]
    sigma_out[...] = sigma[...]


def body(n, energies, retarded, contact, atom_kind, coupling, shifts):
    rows, columns = retarded.shape[2:]
    L = rows // B
    NB = n * L
    X = energies // 2
    modes = coupling.shape[1]
    f32, bf16 = jnp.float32, jnp.bfloat16
    out = jax.ShapeDtypeStruct(contact.shape, f32)
    vmem = pl.BlockSpec(memory_space=pltpu.VMEM)
    anywhere = pl.BlockSpec(memory_space=pl.ANY)
    scalars = pl.BlockSpec(memory_space=pltpu.SMEM)
    dma = pltpu.SemaphoreType.DMA
    far = max(X - 1, 1)
    results = pl.pallas_call(
        functools.partial(kernel, n, energies, L, modes),
        out_shape=(out, out, out),
        in_specs=[
            anywhere, anywhere, scalars, scalars, scalars,
        ],
        out_specs=(vmem, vmem, vmem),
        scratch_shapes=[
            pltpu.VMEM((2, rows, columns), f32),
            pltpu.VMEM((NB, L, 2 * B, 2 * B), bf16),
            pltpu.VMEM((NB, L, 2 * B, 2 * B), bf16),
            pltpu.VMEM((modes, L, B, B), f32),
            pltpu.VMEM((NB, B, 2 * B), bf16),
            pltpu.VMEM((NB, B, 2 * B), bf16),
            pltpu.VMEM((ITERS, NB, 2, B, B), f32),
            pltpu.VMEM((NB, 2, B, B), f32),
            pltpu.VMEM((NB, 2, B, B), f32),
            pltpu.VMEM((L, B, 2 * B), f32),
            pltpu.VMEM((L, B, 2 * B), f32),
            pltpu.VMEM((B, 2 * B), f32),
            pltpu.VMEM((B, 2 * B), f32),
            pltpu.VMEM((ITERS, L, B, 2 * B), f32),
            pltpu.VMEM((ITERS, L, B, 2 * B), f32),
            pltpu.VMEM((ITERS, far, L, B, 2 * B), f32),
            pltpu.VMEM((ITERS, far, L, B, 2 * B), f32),
            dma, dma((L,)),
            dma((ITERS, 2, NB)), dma((ITERS, NB)),
            dma((NB,)), dma((NB,)), dma((NB,)), dma((NB,)),
            dma, dma,
            dma((ITERS, L)), dma((ITERS, L)),
            dma((ITERS, far, L)), dma((ITERS, far, L)),
        ],
        compiler_params=pltpu.CompilerParams(
            collective_id=0, has_side_effects=True, vmem_limit_bytes=58 * 2**20
        ),
        cost_estimate=pl.CostEstimate(
            flops=2 * 3 * 20 * rows * columns * B, bytes_accessed=8 * rows * columns,
            transcendentals=0,
        ),
    )(retarded, contact, atom_kind, coupling, shifts)
    return pl.pallas_call(
        place,
        out_shape=(out, out, out),
        in_specs=[vmem] * 3,
        out_specs=(vmem,) * 3,
    )(*results)


def solution(mesh):
    shape = dict(mesh.shape)
    spec = P(None, ("grp", "en"), "pan", None)
    return jax.shard_map(
        functools.partial(body, shape["pan"], shape["en"]),
        mesh=mesh,
        in_specs=(spec, spec, P(), P(), P()),
        out_specs=(spec, spec, spec),
        check_vma=False,
    )
```

```python
import functools
import math

import jax
import jax.numpy as jnp
from jax import lax
from jax.experimental import pallas as pl
from jax.experimental.pallas import tpu as pltpu
from jax.sharding import PartitionSpec as P

B = 128
ORB = 8
ITERS = 2
MESH = pl.DeviceIdType.MESH


def split(x):
    hi = x.astype(jnp.bfloat16)
    return hi, (x - hi.astype(jnp.float32)).astype(jnp.bfloat16)


def nn(a, b):
    return jnp.dot(a, b, preferred_element_type=jnp.float32)


def nt(a, b):
    return lax.dot_general(a, b, (((1,), (1,)), ((), ())), preferred_element_type=jnp.float32)


def three(f, a, b):
    return f(a[0], b[0]) + (f(a[1], b[0]) + f(a[0], b[1]))


def mix(re, im):
    return split(
        jnp.concatenate(
            [jnp.concatenate([re, im], axis=1), jnp.concatenate([-im, re], axis=1)], axis=0
        )
    )


def kernel(
    n, energies, L, modes,
    green, contact, atom_kind, coupling, shifts,
    diag_out, upper_out, sigma_out,
    gst, rhi, rlo, fac, phi, plo, zbuf, gnext, gprev, dacc, uacc, uret, uadd, dbuf, sib, xsend, xrecv,
    gsem, csem, osem, zs, zr, ns, nr, ps, pr, us, ur, ss, sr, xs, xr,
):
    NB = n * L
    rows = L * B
    X = energies // 2
    scale = 1.0 / math.sqrt(B)
    z = lax.axis_index("pan")
    e = lax.axis_index("en")
    x = lax.div(e, 2)
    core = lax.rem(e, 2)
    other = x * 2 + 1 - core

    load = pltpu.make_async_copy(green.at[:, 0], gst, gsem)
    load.start()
    own = [
        pltpu.make_async_copy(
            contact.at[:, 0, pl.ds(b * B, B)], zbuf.at[0, z * L + b], csem.at[b]
        )
        for b in range(L)
    ]
    for copy in own:
        copy.start()

    barrier = pltpu.get_barrier_semaphore()

    @pl.when(z > 0)
    def _():
        pl.semaphore_signal(barrier, inc=1, device_id={"pan": z - 1}, device_id_type=MESH)

    @pl.when(z < n - 1)
    def _():
        pl.semaphore_signal(barrier, inc=1, device_id={"pan": z + 1}, device_id_type=MESH)

    pl.semaphore_signal(barrier, inc=1, device_id={"en": other}, device_id_type=MESH)

    def target(dx):
        return lax.rem(x + dx, X) * 2 + core

    for dx in range(1, X):
        pl.semaphore_signal(barrier, inc=1, device_id={"en": target(dx)}, device_id_type=MESH)

    ends = (z > 0).astype(jnp.int32) + (z < n - 1).astype(jnp.int32)
    pl.semaphore_wait(barrier, X + ends)

    def zcopy(it, k, side):
        return pltpu.make_async_remote_copy(
            src_ref=zbuf.at[it, k], dst_ref=zbuf.at[it, k],
            send_sem=zs.at[it, side, k], recv_sem=zr.at[it, k],
            device_id={"pan": z + 1 - 2 * side}, device_id_type=MESH,
        )

    def send_own(it, b):
        k = z * L + b
        if it == 0:
            own[b].wait()

        @pl.when(z < n - 1)
        def _():
            zcopy(it, k, 0).start()

        @pl.when(z > 0)
        def _():
            zcopy(it, k, 1).start()

    def cols(k):
        return pl.ds(pl.multiple_of(k * B, B), B)

    def cut(p):
        return lax.div(p * NB, max(n - 2, 1)) if n > 2 else p * 0 + NB // 2

    cut_here = cut(z)
    cut_before = cut(jnp.maximum(z - 1, 0))

    def next_copy(k):
        return pltpu.make_async_remote_copy(
            src_ref=gst.at[:, pl.ds(0, B), cols(k)], dst_ref=gnext.at[k],
            send_sem=ns.at[k], recv_sem=nr.at[k],
            device_id={"pan": z - 1}, device_id_type=MESH,
        )

    def prev_copy(k):
        return pltpu.make_async_remote_copy(
            src_ref=gst.at[:, pl.ds(rows - B, B), cols(k)], dst_ref=gprev.at[k],
            send_sem=ps.at[k], recv_sem=pr.at[k],
            device_id={"pan": z + 1}, device_id_type=MESH,
        )

    def next_sent(k):
        return jnp.logical_and(z > 0, k < cut_before)

    def prev_sent(k):
        return jnp.logical_and(z < n - 1, k >= cut_here)

    at_end = ((z == 0) | (z == n - 1)).astype(jnp.int32)

    early = at_end * lax.div(3 * (n - 2) * L, 2) + (1 - at_end) * L

    def paced(it, u):
        fast = jnp.minimum(jnp.maximum(u + 1 - L, 0), early)
        slow = jnp.maximum(u + 1 - (n - 1) * L, 0)
        first = at_end * fast + (1 - at_end) * slow
        if it == 0:
            return jnp.minimum(first, NB)
        return jnp.minimum(early + at_end * jnp.maximum(u + 1 - L, 0) + (1 - at_end) * jnp.maximum(u + 1 - 2 * L, 0), NB)

    def send_edge(begin, end):
        @pl.loop(begin, end)
        def _(i):
            right = cut_here + i

            @pl.when((z > 0) & (i < cut_before))
            def _():
                next_copy(i).start()

            @pl.when((z < n - 1) & (right < NB))
            def _():
                prev_copy(right).start()

    def absorb(it, k):
        if it == 0:
            cat = jnp.concatenate([gst[0, :, cols(k)], gst[1, :, cols(k)]], axis=1)
            hi, lo = split(cat)
            for part, ref in ((hi, rhi), (lo, rlo)):
                ref[k, :, :B, :] = part.reshape(L, B, 2 * B)
                ref[k, :, B:, :] = jnp.concatenate(
                    [-part[:, B:], part[:, :B]], axis=1
                ).reshape(L, B, 2 * B)
            left = (hi, lo)
        else:
            left = tuple(ref[k, :, :B, :].reshape(rows, 2 * B) for ref in (rhi, rlo))
        mixed = mix(zbuf[it, k, 0], zbuf[it, k, 1])
        prod = split(three(nn, left, mixed))
        for j in range(L):
            right = (rhi[k, j], rlo[k, j])
            if it < ITERS - 1 or j == 0:
                got = three(nt, tuple(p[j * B:(j + 1) * B] for p in prod), right)
                dacc[j] += got
            else:
                got = three(nt, tuple(p[(j - 1) * B:(j + 1) * B] for p in prod), right)
                uacc[j - 1] += got[:B]
                dacc[j] += got[B:]
        if it == ITERS - 1:
            phi[k] = prod[0][rows - B:]
            plo[k] = prod[1][rows - B:]

    def edges_before():
        @pl.loop(0, NB)
        def _(k):
            @pl.when((z > 0) & (k >= cut_before))
            def _():
                prev_copy(k).wait_recv()
                edge = split(jnp.concatenate([gprev[k, 0], gprev[k, 1]], axis=1))
                edge = split(three(nn, edge, mix(zbuf[ITERS - 1, k, 0], zbuf[ITERS - 1, k, 1])))
                uret[...] += three(nt, edge, (rhi[k, 0], rlo[k, 0]))

    def edges_after():
        @pl.loop(0, NB)
        def _(k):
            @pl.when((z < n - 1) & (k < cut_here))
            def _():
                next_copy(k).wait_recv()
                gr, gi = gnext[k, 0], gnext[k, 1]
                right = split(
                    jnp.concatenate(
                        [jnp.concatenate([gr, gi], axis=1), jnp.concatenate([-gi, gr], axis=1)],
                        axis=0,
                    )
                )
                uacc[L - 1] += three(nt, (phi[k], plo[k]), right)

    steps = n * L

    def gather(it):
        @pl.loop(0, steps)
        def _(u):
            d = lax.div(u, L)
            b = lax.rem(u, L)

            @pl.loop(0, 2)
            def _(side):
                panel = z - d + side * 2 * d
                valid = (panel >= 0) & (panel < n) & ((d > 0) | (side == 0))
                k = panel * L + b

                @pl.when(valid)
                def _():
                    @pl.when(d > 0)
                    def _():
                        zcopy(it, k, side).wait_recv()
                        onward = z + 1 - 2 * side

                        @pl.when((onward >= 0) & (onward < n))
                        def _():
                            zcopy(it, k, side).start()

                    absorb(it, k)

            begin = paced(it, u - 1)
            if it == ITERS - 1:
                begin = jnp.where(u == 0, paced(0, steps - 1), begin)
            send_edge(begin, paced(it, u))

        if it == ITERS - 1:
            send_edge(paced(it, steps - 1), NB)

    def weight(m, target_energy, source):
        gap = shifts[m]
        hit = (source == target_energy + gap) | (source == target_energy - gap)
        return jnp.where(hit, jnp.float32(1.0), jnp.float32(0.0))

    def factor(b, target_energy, source):
        total = sum(fac[m, b] * weight(m, target_energy, source) for m in range(modes))
        return jnp.concatenate([total, total], axis=1)

    def make_factor():
        per_block = B // ORB
        lane_atom = lax.div(lax.broadcasted_iota(jnp.int32, (ORB, B), 1), ORB)

        @pl.loop(0, L)
        def _(b):
            kinds = [atom_kind[(z * L + b) * per_block + a] for a in range(per_block)]
            for m in range(modes):
                values = [coupling[kind, m] for kind in kinds]
                row = jnp.zeros((ORB, B), jnp.float32)
                for a, value in enumerate(values):
                    row = jnp.where(lane_atom == a, value, row)
                for a, value in enumerate(values):
                    fac[m, b, a * ORB:(a + 1) * ORB, :] = value * row

    def sib_copy(it, b):
        return pltpu.make_async_remote_copy(
            src_ref=dbuf.at[it, b], dst_ref=sib.at[it, b],
            send_sem=ss.at[it, b], recv_sem=sr.at[it, b],
            device_id={"en": other}, device_id_type=MESH,
        )

    def x_copy(it, dx, b):
        return pltpu.make_async_remote_copy(
            src_ref=xsend.at[it, dx - 1, b], dst_ref=xrecv.at[it, dx - 1, b],
            send_sem=xs.at[it, dx - 1, b], recv_sem=xr.at[it, dx - 1, b],
            device_id={"en": target(dx)}, device_id_type=MESH,
        )

    def exchange(it, done, between):
        for b in range(L):
            dbuf[it, b] = dacc[b] * scale
            sib_copy(it, b).start()
        for b in range(L):
            sib_copy(it, b).wait_recv()
            for dx in range(1, X):
                to = target(dx)
                xsend[it, dx - 1, b] = (
                    factor(b, to, e) * dbuf[it, b] + factor(b, to, other) * sib[it, b]
                )
                x_copy(it, dx, b).start()
        between()
        for b in range(L):
            total = factor(b, e, e) * dbuf[it, b] + factor(b, e, other) * sib[it, b]
            for dx in range(1, X):
                x_copy(it, dx, b).wait_recv()
                total = total + xrecv[it, dx - 1, b]
            k = z * L + b
            done(b, zbuf[0, k, 0] + total[:, :B], zbuf[0, k, 1] + total[:, B:])

    for b in range(L):
        send_own(0, b)
    dacc[...] = jnp.zeros_like(dacc)
    uacc[...] = jnp.zeros_like(uacc)
    uret[...] = jnp.zeros_like(uret)
    make_factor()
    load.wait()

    for it in range(ITERS):
        gather(it)
        if it < ITERS - 1:
            def done(b, re, im):
                k = z * L + b
                zbuf[it + 1, k, 0] = re
                zbuf[it + 1, k, 1] = im
                send_own(it + 1, b)

            exchange(it, done, lambda: None)
            dacc[...] = jnp.zeros_like(dacc)

    puts = []

    def put(out, which, block, b):
        for part in range(2):
            copy = pltpu.make_async_copy(
                block.at[:, pl.ds(part * B, B)], out.at[part, 0, pl.ds(b * B, B)],
                osem.at[which, b, part],
            )
            copy.start()
            puts.append(copy)

    back = pltpu.make_async_remote_copy(
        src_ref=uret, dst_ref=uadd, send_sem=us, recv_sem=ur,
        device_id={"pan": z - 1}, device_id_type=MESH,
    )

    def between():
        for b in range(L):
            put(diag_out, 0, dbuf.at[ITERS - 1, b], b)
        for b in range(L - 1):
            uacc[b] = uacc[b] * scale
            put(upper_out, 1, uacc.at[b], b)
        edges_before()

        @pl.when(z > 0)
        def _():
            back.start()

        edges_after()

    def final(b, re, im):
        dacc[b, :, :B] = re
        dacc[b, :, B:] = im
        put(sigma_out, 2, dacc.at[b], b)

    exchange(ITERS - 1, final, between)

    @pl.when(z < n - 1)
    def _():
        back.wait_recv()
        uacc[L - 1] += uadd[...]

    uacc[L - 1] = uacc[L - 1] * scale
    put(upper_out, 1, uacc.at[L - 1], L - 1)

    @pl.when(z > 0)
    def _():
        back.wait_send()

    for it in range(ITERS):
        for b in range(L):
            sib_copy(it, b).wait_send()
            for dx in range(1, X):
                x_copy(it, dx, b).wait_send()

    @pl.loop(0, NB)
    def _(k):
        panel = lax.div(k, L)
        for it in range(ITERS):
            @pl.when((panel <= z) & (z < n - 1))
            def _():
                zcopy(it, k, 0).wait_send()

            @pl.when((panel >= z) & (z > 0))
            def _():
                zcopy(it, k, 1).wait_send()

        @pl.when(next_sent(k))
        def _():
            next_copy(k).wait_send()

        @pl.when(prev_sent(k))
        def _():
            prev_copy(k).wait_send()

    for copy in puts:
        copy.wait()


def place(diag, upper, sigma, diag_out, upper_out, sigma_out):
    diag_out[...] = diag[...]
    upper_out[...] = upper[...]
    sigma_out[...] = sigma[...]


def body(n, energies, retarded, contact, atom_kind, coupling, shifts):
    rows, columns = retarded.shape[2:]
    L = rows // B
    NB = n * L
    X = energies // 2
    modes = coupling.shape[1]
    f32, bf16 = jnp.float32, jnp.bfloat16
    out = jax.ShapeDtypeStruct(contact.shape, f32)
    vmem = pl.BlockSpec(memory_space=pltpu.VMEM)
    anywhere = pl.BlockSpec(memory_space=pl.ANY)
    scalars = pl.BlockSpec(memory_space=pltpu.SMEM)
    dma = pltpu.SemaphoreType.DMA
    far = max(X - 1, 1)
    results = pl.pallas_call(
        functools.partial(kernel, n, energies, L, modes),
        out_shape=(out, out, out),
        in_specs=[
            anywhere, anywhere, scalars, scalars, scalars,
        ],
        out_specs=(anywhere,) * 3,
        scratch_shapes=[
            pltpu.VMEM((2, rows, columns), f32),
            pltpu.VMEM((NB, L, 2 * B, 2 * B), bf16),
            pltpu.VMEM((NB, L, 2 * B, 2 * B), bf16),
            pltpu.VMEM((modes, L, B, B), f32),
            pltpu.VMEM((NB, B, 2 * B), bf16),
            pltpu.VMEM((NB, B, 2 * B), bf16),
            pltpu.VMEM((ITERS, NB, 2, B, B), f32),
            pltpu.VMEM((NB, 2, B, B), f32),
            pltpu.VMEM((NB, 2, B, B), f32),
            pltpu.VMEM((L, B, 2 * B), f32),
            pltpu.VMEM((L, B, 2 * B), f32),
            pltpu.VMEM((B, 2 * B), f32),
            pltpu.VMEM((B, 2 * B), f32),
            pltpu.VMEM((ITERS, L, B, 2 * B), f32),
            pltpu.VMEM((ITERS, L, B, 2 * B), f32),
            pltpu.VMEM((ITERS, far, L, B, 2 * B), f32),
            pltpu.VMEM((ITERS, far, L, B, 2 * B), f32),
            dma, dma((L,)), dma((3, L, 2)),
            dma((ITERS, 2, NB)), dma((ITERS, NB)),
            dma((NB,)), dma((NB,)), dma((NB,)), dma((NB,)),
            dma, dma,
            dma((ITERS, L)), dma((ITERS, L)),
            dma((ITERS, far, L)), dma((ITERS, far, L)),
        ],
        compiler_params=pltpu.CompilerParams(
            collective_id=0, has_side_effects=True, vmem_limit_bytes=58 * 2**20
        ),
        cost_estimate=pl.CostEstimate(
            flops=2 * 3 * 20 * rows * columns * B, bytes_accessed=8 * rows * columns,
            transcendentals=0,
        ),
    )(retarded, contact, atom_kind, coupling, shifts)
    return pl.pallas_call(
        place,
        out_shape=(out, out, out),
        in_specs=[vmem] * 3,
        out_specs=(vmem,) * 3,
    )(*results)


def solution(mesh):
    shape = dict(mesh.shape)
    spec = P(None, ("grp", "en"), "pan", None)
    return jax.shard_map(
        functools.partial(body, shape["pan"], shape["en"]),
        mesh=mesh,
        in_specs=(spec, spec, P(), P(), P()),
        out_specs=(spec, spec, spec),
        check_vma=False,
    )
```
